1024 devices in a mesh: section: 2 (over z_hi), tensor: 64 (over y, x), dp: 8 (over z_lo, core).
Axes of the slice: x: 8, y: 8, z: 8 (z_hi: 2, z_lo: 4; z = z_hi * 4 + z_lo), core: 2. Of those that a mesh axis runs over, the one named last changes fastest.
Arguments:
- tokens: bfloat16 [1024, 4096], P('dp', 'tensor'), may hold values from -6 to 6
- section_weights: bfloat16 [2, 4096, 14336], P('section', None, 'tensor'), may hold values from -0.09375 to 0.09375
- up_weight: bfloat16 [4096, 14336], P(None, 'tensor'), may hold values from -0.09375 to 0.09375
- cotangent: bfloat16 [1024, 4096], P('dp'), may hold values from -0.1796875 to 0.1796875
Outputs:
- section_grads: bfloat16 [2, 4096, 14336], P('section', 'dp', 'tensor')
- up_grads: bfloat16 [4096, 14336], P(('section', 'dp'), 'tensor')
The draws below stay inside these ranges and needn't reach their ends.
All inputs are finite; a program needn't handle non-finite values.
Results may differ from the reference program's by a relative error of at most 0.018.
Values may be sent and summed in bfloat16 or wider, within the bound.
A program may use at most 32 MiB of HBM per device.

```python
import jax
import jax.numpy as jnp
from jax import lax

D = 4096
FFW = 14336
ROWS = 128
TOKENS = 1024
N_DP = 8


def level_of(own_key, extent, shards, least, high):
    def one(axis_at, parts):
        steps = jax.random.uniform(jax.random.fold_in(jax.random.fold_in(own_key, 6), axis_at), (parts,), jnp.float32, least / len(shards), high / len(shards))
        return jnp.repeat(jnp.exp(steps), extent[axis_at] // parts).reshape((-1,) + (1,) * (len(extent) - axis_at - 1))

    loudness = one(*shards[0])
    for cut in shards[1:]:
        loudness = loudness * one(*cut)
    return loudness


def normal_values(own_key, extent, spread, reach, pieces=(), kind=jnp.bfloat16):
    factor_of = level_of(own_key, extent, pieces, -0.22, 0.18) if pieces else 1.0
    result = jax.random.normal(own_key, extent, jnp.float32) * spread * factor_of
    return jnp.minimum(jnp.maximum(result, -reach), reach).astype(kind)


def setup_inputs(seed: int = 0) -> dict:
    key_of = jax.random.split(jax.random.key(seed), 5)
    return {
        "tokens": normal_values(key_of[0], (TOKENS, D), 1.0, 6.0, ((0, 8), (1, 64))),
        "section_weights": normal_values(key_of[1], (2, D, FFW), D ** -0.5, 0.09375, ((0, 2), (2, 64))),
        "up_weight": normal_values(key_of[2], (D, FFW), D ** -0.5, 0.09375, ((1, 64),)),
        "cotangent": normal_values(key_of[3], (TOKENS, D), 0.03, 0.1796875, ((0, 8),)),
    }


def along_rows(left, right):
    return lax.dot_general(left, right, (((0,), (0,)), ((), ())), preferred_element_type=jnp.float32)


def reference(tokens, section_weights, up_weight, cotangent):
    gate_weight = section_weights[0]
    down_trans = section_weights[1]
    token_groups = tokens.reshape(N_DP, ROWS, D)
    incoming_groups = cotangent.reshape(N_DP, ROWS, D)

    def group_step(carry, pair):
        token_rows, incoming = pair
        gate_pre = jnp.dot(token_rows, gate_weight, preferred_element_type=jnp.float32)
        up_pre = jnp.dot(token_rows, up_weight, preferred_element_type=jnp.float32)
        sigmoid_gate = jax.nn.sigmoid(gate_pre)
        hidden = (gate_pre * sigmoid_gate * up_pre).astype(jnp.bfloat16)
        grad_hidden = jnp.dot(incoming, down_trans, preferred_element_type=jnp.float32)
        grad_gate = (grad_hidden * up_pre * sigmoid_gate * (1.0 + gate_pre * (1.0 - sigmoid_gate))).astype(jnp.bfloat16)
        grad_up = (grad_hidden * gate_pre * sigmoid_gate).astype(jnp.bfloat16)
        gate_part = along_rows(token_rows, grad_gate).astype(jnp.bfloat16)
        down_part = along_rows(incoming, hidden).astype(jnp.bfloat16)
        up_part = along_rows(token_rows, grad_up).astype(jnp.bfloat16)
        gate_part, down_part, up_part = lax.optimization_barrier((gate_part, down_part, up_part))
        gate_sum, down_sum, up_sum = carry
        return (gate_sum + gate_part.astype(jnp.float32), down_sum + down_part.astype(jnp.float32), up_sum + up_part.astype(jnp.float32)), None

    zeros = jnp.zeros((D, FFW), jnp.float32)
    (gate_sum, down_sum, up_sum), _ = lax.scan(group_step, (zeros, zeros, zeros), (token_groups, incoming_groups))
    return jnp.stack([gate_sum, down_sum]).astype(jnp.bfloat16), up_sum.astype(jnp.bfloat16)
```

```python
import jax
import jax.numpy as jnp
from jax import lax
from jax.experimental import pallas as pl
from jax.experimental.pallas import tpu as pltpu
from jax.sharding import PartitionSpec as P

MESH = pl.DeviceIdType.MESH
BF, F32 = jnp.bfloat16, jnp.float32
NT = (((1,), (1,)), ((), ()))


def mod8(v):
    return lax.rem(v + 16, 8)


def kernel(
    tok, slot_w, up_w, cot,
    out_slot, out_up,
    x1, x2, units, wf, wd, cot_v, cot_t, res_slot, res_up,
    load_sem, local_sem,
    p1_send, p1_recv, ring_send, ring_recv,
    perm_send, perm_recv, scat_send,
    gh_send, gh_recv, ghs_send, ghs_recv,
    z_send, z_recv, sib_send, sib_recv,
):
    s = lax.axis_index("section")
    t = lax.axis_index("tensor")
    dp = lax.axis_index("dp")
    y, x = t // 8, lax.rem(t, 8)
    zl, core = dp // 2, lax.rem(dp, 2)
    z = s * 4 + zl
    sib = {"dp": zl * 2 + 1 - core}
    even = core == 0
    o_me = jnp.where(even, y, x)
    i_me = jnp.where(even, x, y)
    so = jnp.where(even, 8, 1)
    si = jnp.where(even, 1, 8)

    def inner_dev(i):
        return {"tensor": o_me * so + i * si}

    def outer_dev(o):
        return {"tensor": o * so + i_me * si}

    def z_dev(zz, c=core):
        return {"section": zz // 4, "dp": lax.rem(zz, 4) * 2 + c}

    def remote(src, dst, ss, rs, dev):
        return pltpu.make_async_remote_copy(
            src_ref=src, dst_ref=dst, send_sem=ss, recv_sem=rs,
            device_id=dev, device_id_type=MESH,
        )

    own1 = x1.at[o_me, i_me]
    ld_tok = pltpu.make_async_copy(tok, own1, load_sem.at[0])
    ld_tok.start()

    @pl.when(s == 0)
    def _():
        pltpu.make_async_copy(slot_w, wf, load_sem.at[1]).start()

    @pl.when(s == 1)
    def _():
        pltpu.make_async_copy(slot_w, wd, load_sem.at[2]).start()
        pltpu.make_async_copy(cot, cot_v, load_sem.at[3]).start()
        pltpu.make_async_copy(up_w, wf, load_sem.at[1]).start()

    perm_t, perm_d = dp * 8 + x, y
    has_perm = jnp.logical_and(s == 0, y != dp)
    up_src_y = s * 4 + dp // 2
    up_src_x = lax.rem(dp, 2) * 4 + x // 2
    up_src_t = up_src_y * 8 + up_src_x
    up_src_self = jnp.logical_and(up_src_t == t, y == dp)
    up_sends = y // 4 == s
    up_dst_d = lax.rem(y, 4) * 2 + x // 4
    up_dst_x = [lax.rem(x, 4) * 2 + h for h in range(2)]
    up_dst_t = [dp * 8 + v for v in up_dst_x]
    up_dst_self = [jnp.logical_and(v == t, up_dst_d == dp) for v in up_dst_t]

    barrier = pltpu.get_barrier_semaphore()

    def greet(dev):
        pl.semaphore_signal(barrier, inc=1, device_id=dev, device_id_type=MESH)

    for k in range(1, 8):
        greet(inner_dev(mod8(i_me + k)))
    greet(outer_dev(mod8(o_me + 1)))
    greet(outer_dev(mod8(o_me - 1)))
    for k in range(1, 8):
        greet(z_dev(mod8(z + k)))
        greet(z_dev(mod8(z + k), 1 - core))
    greet(sib)

    @pl.when(has_perm)
    def _():
        greet({"tensor": perm_t, "dp": perm_d})

    @pl.when(jnp.logical_not(up_src_self))
    def _():
        greet({"tensor": up_src_t, "dp": y})

    ld_tok.wait()
    expected = 7 + 2 + 15 + has_perm.astype(jnp.int32)
    for h in range(2):
        expected += jnp.logical_and(up_sends, jnp.logical_not(up_dst_self[h])).astype(jnp.int32)
    pl.semaphore_wait(barrier, expected)

    def p1_copy(buf, n, k):
        own = buf.at[o_me, i_me]
        return remote(own, own, p1_send.at[n, k - 1], p1_recv.at[n, k - 1],
                      inner_dev(mod8(i_me + k)))

    def ring_copy(buf, n, way, d, c):
        sign = 1 if way == 0 else -1
        block = mod8(o_me - sign * (d - 1))
        part = buf.at[block, pl.ds(2 * c, 2)]
        at = (d - 1) * 4 + c
        return remote(part, part, ring_send.at[n, way, at], ring_recv.at[n, way, at],
                      outer_dev(mod8(o_me + sign)))

    def ring_chunks(way, d):
        if d < 4:
            return range(4)
        return range(2) if way == 0 else range(2, 4)

    def p1_start(buf, n):
        for k in range(1, 8):
            p1_copy(buf, n, k).start()

    def p1_wait(buf, n):
        for k in range(1, 8):
            p1_copy(buf, n, k).wait_recv()

    def ring_step(buf, n, d):
        for c in range(4):
            for way in range(2):
                if c in ring_chunks(way, d):
                    if d > 1:
                        ring_copy(buf, n, way, d - 1, c).wait_recv()
                    ring_copy(buf, n, way, d, c).start()

    def ring_rest(buf, n):
        for c in range(4):
            for way in range(2):
                if c not in ring_chunks(way, 4):
                    ring_copy(buf, n, way, 3, c).wait_recv()
                else:
                    ring_copy(buf, n, way, 4, c).wait_recv()

    def all_sends(buf, n):
        for k in range(1, 8):
            p1_copy(buf, n, k).wait_send()
        for d in range(1, 5):
            for way in range(2):
                for c in ring_chunks(way, d):
                    ring_copy(buf, n, way, d, c).wait_send()

    p1_start(x1, 0)

    own2 = x2.at[o_me, i_me]

    def slot_at(d_core, yy, xx):
        return jnp.where(d_core == 0, yy, xx), jnp.where(d_core == 0, xx, yy)

    def perm_copy():
        a, b = slot_at(lax.rem(y, 2), dp, x)
        return remote(own1, x2.at[a, b, pl.ds(0, 64)], perm_send.at[0], perm_recv.at[0],
                      {"tensor": perm_t, "dp": perm_d})

    def up_copy(h):
        a, b = slot_at(lax.rem(up_dst_d, 2), dp, up_dst_x[h])
        return remote(own1.at[pl.ds(32 * h, 32)], x2.at[a, b, pl.ds(64, 32)],
                      perm_send.at[1 + h], perm_recv.at[1],
                      {"tensor": up_dst_t[h], "dp": up_dst_d})

    def perm_local():
        return pltpu.make_async_copy(own1, own2.at[pl.ds(0, 64)], local_sem.at[0])

    def up_local(h):
        return pltpu.make_async_copy(own1.at[pl.ds(32 * h, 32)], own2.at[pl.ds(64, 32)], local_sem.at[1])

    @pl.when(has_perm)
    def _():
        perm_copy().start()

    @pl.when(jnp.logical_and(s == 0, y == dp))
    def _():
        perm_local().start()

    for h in range(2):
        @pl.when(jnp.logical_and(up_sends, jnp.logical_not(up_dst_self[h])))
        def _():
            up_copy(h).start()

        @pl.when(jnp.logical_and(up_sends, up_dst_self[h]))
        def _():
            up_local(h).start()

    odd_rows = pl.ds(pl.multiple_of(lax.rem(x, 2) * 64, 64), 64)

    def scat_slot(g):
        a, b = (y, x) if g % 2 == 0 else (x, y)
        return x2.at[a, b, pl.ds(0, 64)]

    def scat_copy(g):
        return remote(cot_t.at[g, odd_rows], scat_slot(g), scat_send.at[g], perm_recv.at[0], {"dp": g})

    def scat_local(g):
        return pltpu.make_async_copy(cot_t.at[g, odd_rows], scat_slot(g), local_sem.at[0])

    is_scat = jnp.logical_and(s == 1, y == dp)

    def gh_copy(k):
        unit = units.at[2, dp]
        return remote(unit, unit, gh_send.at[k - 1], gh_recv.at[zl], z_dev(mod8(z + k)))

    def gh_sib(q):
        unit = units.at[2, q * 2 + core]
        return remote(unit, unit, ghs_send.at[q], ghs_recv.at[q], sib)

    @pl.when(s == 1)
    def _():
        pltpu.make_async_copy(slot_w, wd, load_sem.at[2]).wait()
        pltpu.make_async_copy(cot, cot_v, load_sem.at[3]).wait()

    @pl.when(is_scat)
    def _():
        for g in range(8):
            lanes = pl.ds(pl.multiple_of(g * 512 + (x // 2) * 128, 128), 128)
            cot_t[g] = cot_v[:, lanes].T
        for g in range(8):
            @pl.when(dp != g)
            def _():
                scat_copy(g).start()

            @pl.when(dp == g)
            def _():
                scat_local(g).start()

    @pl.when(s == 1)
    def _():
        gh = lax.dot_general(wd[...], cot_v[...], NT, preferred_element_type=F32)
        units[2, dp] = gh.astype(BF)
        for k in range(1, 8):
            gh_copy(k).start()

    p1_wait(x1, 0)
    ring_step(x1, 0, 1)

    @pl.when(jnp.logical_or(has_perm, jnp.logical_and(s == 1, y != dp)))
    def _():
        perm_copy().wait_recv()

    @pl.when(y == dp)
    def _():
        perm_local().wait()

    @pl.when(jnp.logical_not(up_src_self))
    def _():
        up_copy(0).wait_recv()

    @pl.when(up_src_self)
    def _():
        up_local(0).wait()

    ring_step(x1, 0, 2)
    p1_start(x2, 1)
    ring_step(x1, 0, 3)
    ring_step(x1, 0, 4)

    for q in range(4):
        @pl.when(jnp.logical_or(s == 0, zl != q))
        def _():
            unit = units.at[2, q * 2 + core]
            remote(unit, unit, gh_send.at[0], gh_recv.at[q], sib).wait_recv()
        gh_sib(q).start()

    p1_wait(x2, 1)
    ring_step(x2, 1, 1)
    ring_rest(x1, 0)

    @pl.when(s == 0)
    def _():
        pltpu.make_async_copy(slot_w, wf, load_sem.at[1]).wait()

    @pl.when(s == 1)
    def _():
        pltpu.make_async_copy(up_w, wf, load_sem.at[1]).wait()

    def piece1(yy, xx):
        a, b = slot_at(core, yy, xx)
        return x1[a, b]

    pre = jnp.zeros((224, 128), F32)
    for yy in range(8):
        rows = jnp.concatenate([piece1(yy, xx) for xx in range(8)], axis=0)
        pre += jnp.dot(wf[:, yy * 512 : yy * 512 + 512], rows, preferred_element_type=F32)
    units[s, dp] = pre.astype(BF)

    def z_unit(zz):
        return units.at[zz // 4, lax.rem(zz, 4) * 2 + core]

    def z_copy(way, d, c):
        sign = 1 if way == 0 else -1
        part = z_unit(mod8(z - sign * (d - 1))).at[pl.ds(112 * c, 112)]
        at = (d - 1) * 2 + c
        return remote(part, part, z_send.at[way, at], z_recv.at[way, at], z_dev(mod8(z + sign)))

    def z_chunks(way, d):
        if d < 4:
            return range(2)
        return range(1) if way == 0 else range(1, 2)

    def z_sib(k):
        unit = z_unit(mod8(z + k))
        return remote(unit, unit, sib_send.at[k], sib_recv.at[k], sib)

    def z_step(d):
        for c in range(2):
            for way in range(2):
                if d > 1:
                    z_copy(way, d - 1, c).wait_recv()
                if c in z_chunks(way, d):
                    z_copy(way, d, c).start()

    z_step(1)
    z_sib(0).start()
    ring_step(x2, 1, 2)
    z_step(2)
    z_sib(7).start()
    z_sib(1).start()
    ring_step(x2, 1, 3)
    z_step(3)
    z_sib(6).start()
    z_sib(2).start()
    ring_step(x2, 1, 4)
    z_step(4)
    z_sib(5).start()
    z_sib(3).start()
    z_copy(0, 4, 0).wait_recv()
    z_copy(1, 4, 1).wait_recv()
    z_sib(4).start()

    for q in range(4):
        gh_sib(q).wait_recv()
    for k in range(8):
        z_sib(k).wait_recv()
    ring_rest(x2, 1)

    total_slot = jnp.zeros((224, 512), F32)
    total_up = jnp.zeros((224, 256), F32)

    def piece2(g, xx):
        a, b = slot_at(core, g, xx)
        return x2[a, b]

    is_first = s == 0
    for pair in range(4):
        lefts, ups, rows_slot, rows_up = [], [], [], []
        for g in (2 * pair, 2 * pair + 1):
            gate = units[0, g].astype(F32)
            up = units[1, g].astype(F32)
            gh = units[2, g].astype(F32)
            sg = jax.nn.sigmoid(gate)
            act = gate * sg
            lefts.append(jnp.where(
                is_first, gh * up * sg * (1.0 + gate * (1.0 - sg)), act * up).astype(BF))
            ups.append((gh * act).astype(BF))
            pieces = [piece2(g, xx) for xx in range(8)]
            rows_slot.append(jnp.concatenate([v[:64] for v in pieces], axis=0))
            rows_up.append(jnp.concatenate([v[64:] for v in pieces], axis=0))
        total_slot += lax.dot_general(
            jnp.concatenate(lefts, axis=1), jnp.concatenate(rows_slot, axis=1), NT,
            preferred_element_type=F32)
        total_up += lax.dot_general(
            jnp.concatenate(ups, axis=1), jnp.concatenate(rows_up, axis=1), NT,
            preferred_element_type=F32)
    res_slot[...] = total_slot.astype(BF)
    res_up[...] = total_up.astype(BF)
    st_slot = pltpu.make_async_copy(res_slot, out_slot, load_sem.at[0])
    st_up = pltpu.make_async_copy(res_up, out_up, load_sem.at[1])
    st_slot.start()
    st_up.start()

    all_sends(x1, 0)
    all_sends(x2, 1)

    @pl.when(has_perm)
    def _():
        perm_copy().wait_send()

    for h in range(2):
        @pl.when(jnp.logical_and(up_sends, jnp.logical_not(up_dst_self[h])))
        def _():
            up_copy(h).wait_send()

    @pl.when(is_scat)
    def _():
        for g in range(8):
            @pl.when(dp != g)
            def _():
                scat_copy(g).wait_send()

    @pl.when(s == 1)
    def _():
        for k in range(1, 8):
            gh_copy(k).wait_send()

    for q in range(4):
        gh_sib(q).wait_send()
    for k in range(8):
        z_sib(k).wait_send()
    for way in range(2):
        for d in range(1, 5):
            for c in z_chunks(way, d):
                z_copy(way, d, c).wait_send()
    st_slot.wait()
    st_up.wait()


def local(tokens, section_weights, up_weight, cotangent):
    dma = pltpu.SemaphoreType.DMA
    any_spec = pl.BlockSpec(memory_space=pl.ANY)
    slot_t, up_t = pl.pallas_call(
        kernel,
        out_shape=(jax.ShapeDtypeStruct((224, 512), BF), jax.ShapeDtypeStruct((224, 256), BF)),
        in_specs=[any_spec] * 4,
        out_specs=(any_spec, any_spec),
        scratch_shapes=[
            pltpu.VMEM((8, 8, 64, 128), BF),
            pltpu.VMEM((8, 8, 96, 128), BF),
            pltpu.VMEM((3, 8, 224, 128), BF),
            pltpu.VMEM((224, 4096), BF),
            pltpu.VMEM((224, 4096), BF),
            pltpu.VMEM((128, 4096), BF),
            pltpu.VMEM((8, 128, 128), BF),
            pltpu.VMEM((224, 512), BF),
            pltpu.VMEM((224, 256), BF),
            dma((4,)), dma((2,)),
            dma((2, 7)), dma((2, 7)), dma((2, 2, 16)), dma((2, 2, 16)),
            dma((3,)), dma((2,)), dma((8,)),
            dma((7,)), dma((4,)), dma((4,)), dma((4,)),
            dma((2, 8)), dma((2, 8)), dma((8,)), dma((8,)),
        ],
        compiler_params=pltpu.CompilerParams(
            collective_id=0, has_side_effects=True, vmem_limit_bytes=40 * 1024 * 1024
        ),
        cost_estimate=pl.CostEstimate(flops=10**9, bytes_accessed=10**7, transcendentals=10**6),
    )(tokens.T, section_weights[0].T, up_weight.T, cotangent)
    return slot_t.T[None], up_t.T


def solution(mesh):
    placed = (P("dp", "tensor"), P("section", None, "tensor"), P(None, "tensor"), P("dp", None))
    return jax.shard_map(
        local,
        mesh=mesh,
        in_specs=placed,
        out_specs=(P("section", "dp", "tensor"), P(("section", "dp"), "tensor")),
        check_vma=False,
    )
```

```python
import jax
import jax.numpy as jnp
from jax import lax
from jax.experimental import pallas as pl
from jax.experimental.pallas import tpu as pltpu
from jax.sharding import PartitionSpec as P

MESH = pl.DeviceIdType.MESH
BF, F32, I32 = jnp.bfloat16, jnp.float32, jnp.int32
NT = (((1,), (1,)), ((), ()))


def mod8(v):
    return lax.rem(v + 16, 8)


def both(*conditions):
    out = conditions[0]
    for c in conditions[1:]:
        out = jnp.logical_and(out, c)
    return out


def kernel(
    tok, slot_w, up_w, cot,
    out_slot, out_up,
    x1, x2, x3, units, gh_v, wf, wd, cot_v, cot_t, res_slot, res_up,
    load_sem, local_sem, ready0, ready1,
    p1_send, p1_recv, ring_send, ring_recv,
    perm_send, perm_recv, scat_send, scat_recv,
    gh_send, gh_recv,
    z_send, z_recv, sib_send, sib_recv,
):
    s = lax.axis_index("section")
    t = lax.axis_index("tensor")
    dp = lax.axis_index("dp")
    y, x = t // 8, lax.rem(t, 8)
    zl, core = dp // 2, lax.rem(dp, 2)
    z = s * 4 + zl
    first, second = s == 0, s == 1
    sib = {"dp": zl * 2 + 1 - core}
    even = core == 0
    o_me = jnp.where(even, y, x)
    i_me = jnp.where(even, x, y)
    so = jnp.where(even, 8, 1)
    si = jnp.where(even, 1, 8)

    def when(*conditions):
        return pl.when(both(*conditions))

    def count(*conditions):
        return both(*conditions).astype(I32)

    def inner_dev(i):
        return {"tensor": o_me * so + i * si}

    def outer_dev(o):
        return {"tensor": o * so + i_me * si}

    def z_dev(zz, c=core):
        return {"section": zz // 4, "dp": lax.rem(zz, 4) * 2 + c}

    def remote(src, dst, ss, rs, dev):
        return pltpu.make_async_remote_copy(
            src_ref=src, dst_ref=dst, send_sem=ss, recv_sem=rs,
            device_id=dev, device_id_type=MESH,
        )

    def slot_at(d_core, yy, xx):
        return jnp.where(d_core == 0, yy, xx), jnp.where(d_core == 0, xx, yy)

    own1, own2, own3 = x1.at[o_me, i_me], x2.at[o_me, i_me], x3.at[o_me, i_me]
    ld_tok = pltpu.make_async_copy(tok, own1, load_sem.at[0])
    ld_tok.start()

    @when(first)
    def _():
        pltpu.make_async_copy(slot_w, wf, load_sem.at[1]).start()
        pltpu.make_async_copy(up_w, wd, load_sem.at[2]).start()

    @when(second)
    def _():
        pltpu.make_async_copy(cot, cot_v, load_sem.at[3]).start()
        pltpu.make_async_copy(slot_w, wd, load_sem.at[2]).start()

    perm_t, perm_d = dp * 8 + x, y
    perm_z = y // 2
    has_perm = both(first, y != dp)
    up_src_t = (s * 4 + dp // 2) * 8 + lax.rem(dp, 2) * 4 + x // 2
    up_src_z = y // 2
    up_recvs = jnp.logical_not(both(up_src_t == t, y == dp))
    up_dst_d = lax.rem(y, 4) * 2 + x // 4
    up_dst_z = up_dst_d // 2
    up_dst_x = [lax.rem(x, 4) * 2 + h for h in range(2)]
    up_dst_t = [dp * 8 + v for v in up_dst_x]
    up_from = y // 4 == s
    up_self = [both(up_from, v == t, up_dst_d == dp) for v in up_dst_t]
    up_sends = [both(up_from, jnp.logical_not(v)) for v in up_self]

    barrier = pltpu.get_barrier_semaphore()

    def tell(sem, dev):
        pl.semaphore_signal(sem, inc=1, device_id=dev, device_id_type=MESH)

    def wait_for(sem, number):
        @when(number > 0)
        def _():
            pl.semaphore_wait(sem, number)

    def answer(dev):
        @when(first)
        def _():
            tell(ready0, dev)

        @when(second)
        def _():
            tell(ready1, dev)

    for k in range(1, 8):
        tell(barrier, inner_dev(mod8(i_me + k)))
    for k in (1, -1, 2, -2):
        tell(barrier, outer_dev(mod8(o_me + k)))
    tell(barrier, sib)

    @when(first)
    def _():
        tell(barrier, {"section": 1})

    @when(first, jnp.logical_or(zl == 0, zl == 3))
    def _():
        tell(barrier, {"section": 1, "dp": (3 - zl) * 2 + core})

    @when(first, zl < 3)
    def _():
        tell(barrier, {"dp": dp + 2})

    for q in range(1, 4):
        @when(second, zl < q)
        def _():
            tell(barrier, {"dp": 2 * q})
            tell(barrier, {"dp": 2 * q + 1})

    @when(has_perm, perm_z >= zl)
    def _():
        tell(barrier, {"tensor": perm_t, "dp": perm_d})

    @when(up_recvs, up_src_z >= zl)
    def _():
        tell(barrier, {"tensor": up_src_t, "dp": y})

    for h in range(2):
        @when(up_sends[h], up_dst_z > zl)
        def _():
            tell(barrier, {"tensor": up_dst_t[h], "dp": up_dst_d})

    expected = 12 + count(first, zl > 0) + jnp.where(second, 1 + 2 * zl, 0)
    expected += count(second, jnp.logical_or(zl == 0, zl == 3))
    expected += count(has_perm, perm_z <= zl) + count(up_recvs, up_src_z < zl)
    for h in range(2):
        expected += count(up_sends[h], up_dst_z <= zl)

    half = pl.ds(pl.multiple_of(lax.rem(y, 2) * 64, 64), 64), pl.ds(pl.multiple_of(lax.rem(x, 2) * 64, 64), 64)

    @when(second)
    def _():
        pltpu.make_async_copy(cot, cot_v, load_sem.at[3]).wait()
        for g in range(8):
            pos = y if g % 2 == 0 else x
            lanes = pl.ds(pl.multiple_of(g * 512 + (pos // 2) * 128, 128), 128)
            cot_t[g] = cot_v[:, lanes].T
        pltpu.make_async_copy(slot_w, wd, load_sem.at[2]).wait()
        gh = lax.dot_general(wd[...], cot_v[...], NT, preferred_element_type=F32)
        gh_v[...] = gh.astype(BF)

    ld_tok.wait()
    pl.semaphore_wait(barrier, expected)

    @when(first, zl > 0)
    def _():
        tell(ready0, {"dp": dp - 2})

    for q in range(3):
        @when(second, zl > q)
        def _():
            tell(ready1, {"dp": 2 * q})
            tell(ready1, {"dp": 2 * q + 1})

    @when(second, jnp.logical_or(zl == 0, zl == 3))
    def _():
        tell(ready1, {"section": 0, "dp": (3 - zl) * 2 + core})

    @when(has_perm, perm_z < zl)
    def _():
        tell(ready0, {"tensor": perm_t, "dp": perm_d})

    @when(up_recvs, up_src_z < zl)
    def _():
        answer({"tensor": up_src_t, "dp": y})

    ups_above = count(up_sends[0], up_dst_z > zl) + count(up_sends[1], up_dst_z > zl)

    def p1_copy(buf, n, k):
        own = buf.at[o_me, i_me]
        return remote(own, own, p1_send.at[n, k - 1], p1_recv.at[n, k - 1],
                      inner_dev(mod8(i_me + k)))

    def ring_copy(buf, n, way, at):
        sign = 1 if way == 0 else -1
        part = buf.at[mod8(o_me - (0 if at < 2 else 2 * sign))]
        if at == 3:
            part = part.at[pl.ds(4 * way, 4)]
        return remote(part, part, ring_send.at[n, way, at], ring_recv.at[n, way, at],
                      outer_dev(mod8(o_me + sign * (1 + at % 2))))

    def p1_start(buf, n):
        for k in range(1, 8):
            p1_copy(buf, n, k).start()

    def p1_wait(buf, n):
        for k in range(1, 8):
            p1_copy(buf, n, k).wait_recv()

    def ring_first(buf, n):
        for at in (1, 0):
            for way in range(2):
                ring_copy(buf, n, way, at).start()

    def ring_second(buf, n):
        for way in range(2):
            ring_copy(buf, n, way, 1).wait_recv()
            ring_copy(buf, n, way, 3).start()
            ring_copy(buf, n, way, 2).start()

    def ring_rest(buf, n):
        for at in (0, 2, 3):
            for way in range(2):
                ring_copy(buf, n, way, at).wait_recv()

    def p1_sent(buf, n):
        for k in range(1, 8):
            p1_copy(buf, n, k).wait_send()

    def ring_sent(buf, n):
        for at in range(4):
            for way in range(2):
                ring_copy(buf, n, way, at).wait_send()

    def perm_copy():
        a, b = slot_at(lax.rem(y, 2), dp, x)
        return remote(own1, x2.at[a, b], perm_send.at[0], perm_recv.at[0],
                      {"tensor": perm_t, "dp": perm_d})

    def up_copy(h):
        a, b = slot_at(lax.rem(up_dst_d, 2), dp, up_dst_x[h])
        return remote(own1.at[pl.ds(32 * h, 32)], x3.at[a, b],
                      perm_send.at[1 + h], perm_recv.at[1],
                      {"tensor": up_dst_t[h], "dp": up_dst_d})

    def perm_local():
        return pltpu.make_async_copy(own1, own2, local_sem.at[0])

    def up_local(h):
        return pltpu.make_async_copy(own1.at[pl.ds(32 * h, 32)], own3, local_sem.at[1])

    def up_start():
        for h in range(2):
            @when(up_sends[h])
            def _():
                up_copy(h).start()

            @when(up_self[h])
            def _():
                up_local(h).start()

    def up_wait():
        @when(up_recvs)
        def _():
            up_copy(0).wait_recv()

        @when(jnp.logical_not(up_recvs))
        def _():
            up_local(0).wait()

    def scat_copy(g):
        place = x2.at[y if g % 2 == 0 else x, dp]
        return remote(cot_t.at[g, half[g % 2]], place, scat_send.at[g], scat_recv.at[dp], {"dp": g})

    def scat_local(g):
        place = x2.at[y if g % 2 == 0 else x, dp]
        return pltpu.make_async_copy(cot_t.at[g, half[g % 2]], place, local_sem.at[0])

    def scat_arrived(g):
        place = x2.at[o_me, g]
        return remote(place, place, scat_send.at[g], scat_recv.at[g], sib)

    def gh_copy():
        return remote(gh_v, gh_v, gh_send, gh_recv, {"section": 0})

    def z_rides(way, d, c, to):
        if way == 0:
            src = to - d
            ok = both(src >= 0, src < 4, jnp.logical_or(to < 4, src >= 2))
            on = src >= 2
        else:
            src = mod8(to + d)
            ok = both(src < 4, jnp.where(to < 4, src > to, src < 2))
            on = src < 2
        return both(ok, to < 4) if c == 0 else ok if c == 1 else both(ok, on)

    def z_copy(way, d, c):
        sign = 1 if way == 0 else -1
        src = mod8(z - sign * (d - 1))
        part = units.at[lax.rem(src, 4) * 2 + core, c]
        return remote(part, part, z_send.at[way, d - 1, c], z_recv.at[way, d - 1, c], z_dev(mod8(z + sign)))

    def z_sends(way, d, c):
        return z_rides(way, d, c, mod8(z + (1 if way == 0 else -1)))

    def z_sib(k, c):
        q = lax.rem(mod8(z + k), 4)
        unit = units.at[q * 2 + core, c]
        return remote(unit, unit, sib_send.at[q, c], sib_recv.at[q, c], sib)

    def z_wanted(c):
        return first if c == 0 else second if c == 2 else jnp.logical_or(first, second)

    def z_step(d):
        for c in (1, 0, 2):
            for way in range(2):
                if d > 1:
                    @when(z_rides(way, d - 1, c, z))
                    def _():
                        z_copy(way, d - 1, c).wait_recv()

                if d < 6:
                    @when(z_sends(way, d, c))
                    def _():
                        z_copy(way, d, c).start()

                if d > 1:
                    @when(z_rides(way, d - 1, c, z), z_wanted(c))
                    def _():
                        z_sib(1 - d if way == 0 else d - 1, c).start()

    @when(first)
    def _():
        p1_start(x1, 0)
        p1_wait(x1, 0)
        ring_first(x1, 0)
        wait_for(ready0, count(zl < 3) + count(has_perm, perm_z > zl) + ups_above)

        @when(has_perm)
        def _():
            perm_copy().start()

        @when(y == dp)
        def _():
            perm_local().start()

        up_start()
        ring_second(x1, 0)

        @when(has_perm)
        def _():
            perm_copy().wait_recv()

        @when(y == dp)
        def _():
            perm_local().wait()

        up_wait()
        p1_start(x2, 1)
        p1_start(x3, 2)
        ring_rest(x1, 0)
        pltpu.make_async_copy(slot_w, wf, load_sem.at[1]).wait()
        pltpu.make_async_copy(up_w, wd, load_sem.at[2]).wait()

        gate_pre = jnp.zeros((224, 128), F32)
        up_pre = jnp.zeros((224, 128), F32)
        for yy in range(8):
            places = [slot_at(core, yy, xx) for xx in range(8)]
            rows = jnp.concatenate([x1[a, b] for a, b in places], axis=0)
            gate_pre += jnp.dot(wf[:, yy * 512 : yy * 512 + 512], rows, preferred_element_type=F32)
            up_pre += jnp.dot(wd[:, yy * 512 : yy * 512 + 512], rows, preferred_element_type=F32)
        gh_copy().wait_recv()
        grad_hidden = gh_v[...].astype(F32)
        sg = jax.nn.sigmoid(gate_pre)
        act = gate_pre * sg
        units[dp, 1] = (grad_hidden * act).astype(BF)
        units[dp, 0] = (grad_hidden * up_pre * sg * (1.0 + gate_pre * (1.0 - sg))).astype(BF)
        units[dp, 2] = (act * up_pre).astype(BF)

        @when(jnp.logical_or(zl == 0, zl == 3))
        def _():
            pl.semaphore_wait(ready1, 1)

        z_step(1)
        z_sib(0, 1).start()
        z_sib(0, 0).start()
        p1_wait(x2, 1)
        ring_first(x2, 1)
        p1_wait(x3, 2)
        ring_first(x3, 2)
        z_step(2)
        ring_second(x2, 1)
        ring_second(x3, 2)
        z_step(3)
        z_step(4)

    @when(second)
    def _():
        gh_copy().start()
        wait_for(ready1, 2 * (3 - zl) + ups_above)
        up_start()
        for g in range(8):
            @when(dp != g)
            def _():
                scat_copy(g).start()

            @when(dp == g)
            def _():
                scat_local(g).start()
        up_wait()
        p1_start(x3, 2)
        for g in range(8):
            @when(dp != g)
            def _():
                scat_arrived(g).wait_recv()

            @when(dp == g)
            def _():
                scat_local(g).wait()
        ring_first(x2, 1)
        p1_wait(x3, 2)
        ring_first(x3, 2)
        ring_second(x2, 1)
        ring_second(x3, 2)
        for d in range(2, 7):
            z_step(d)

    ring_rest(x2, 1)
    ring_rest(x3, 2)
    side = jnp.where(first, 0, 2)
    for q in range(4):
        for c in (1, side):
            unit = units.at[q * 2 + 1 - core, c]
            remote(unit, unit, sib_send.at[q, c], sib_recv.at[q, c], sib).wait_recv()

    total_slot = jnp.zeros((224, 512), F32)
    total_up = jnp.zeros((224, 256), F32)
    by_group = both(first, even)
    for pair in range(4):
        lefts, ups, rows_slot, rows_up = [], [], [], []
        for g in (2 * pair, 2 * pair + 1):
            lefts.append(units[g, side])
            ups.append(units[g, 1])
            rows_slot.append(jnp.concatenate(
                [x2[jnp.where(by_group, g, j), jnp.where(by_group, j, g)] for j in range(8)], axis=0))
            places = [slot_at(core, g, xx) for xx in range(8)]
            rows_up.append(jnp.concatenate([x3[a, b] for a, b in places], axis=0))
        total_slot += lax.dot_general(
            jnp.concatenate(lefts, axis=1), jnp.concatenate(rows_slot, axis=1), NT,
            preferred_element_type=F32)
        total_up += lax.dot_general(
            jnp.concatenate(ups, axis=1), jnp.concatenate(rows_up, axis=1), NT,
            preferred_element_type=F32)
    res_slot[...] = total_slot.astype(BF)
    res_up[...] = total_up.astype(BF)
    st_slot = pltpu.make_async_copy(res_slot, out_slot, load_sem.at[0])
    st_up = pltpu.make_async_copy(res_up, out_up, load_sem.at[1])
    st_slot.start()
    st_up.start()

    @when(first)
    def _():
        p1_sent(x1, 0)
        ring_sent(x1, 0)
        p1_sent(x2, 1)

        @when(has_perm)
        def _():
            perm_copy().wait_send()

    @when(second)
    def _():
        for g in range(8):
            @when(dp != g)
            def _():
                scat_copy(g).wait_send()
        gh_copy().wait_send()

    ring_sent(x2, 1)
    p1_sent(x3, 2)
    ring_sent(x3, 2)
    for h in range(2):
        @when(up_sends[h])
        def _():
            up_copy(h).wait_send()
    for q in range(4):
        for c in (1, side):
            unit = units.at[q * 2 + core, c]
            remote(unit, unit, sib_send.at[q, c], sib_recv.at[q, c], sib).wait_send()
    for way in range(2):
        for d in range(1, 6):
            for c in range(3):
                @when(z_sends(way, d, c))
                def _():
                    z_copy(way, d, c).wait_send()
    st_slot.wait()
    st_up.wait()


def local(tokens, section_weights, up_weight, cotangent):
    dma = pltpu.SemaphoreType.DMA
    any_spec = pl.BlockSpec(memory_space=pl.ANY)
    slot_t, up_t = pl.pallas_call(
        kernel,
        out_shape=(jax.ShapeDtypeStruct((224, 512), BF), jax.ShapeDtypeStruct((224, 256), BF)),
        in_specs=[any_spec] * 4,
        out_specs=(any_spec, any_spec),
        scratch_shapes=[
            pltpu.VMEM((8, 8, 64, 128), BF),
            pltpu.VMEM((8, 8, 64, 128), BF),
            pltpu.VMEM((8, 8, 32, 128), BF),
            pltpu.VMEM((8, 3, 224, 128), BF),
            pltpu.VMEM((224, 128), BF),
            pltpu.VMEM((224, 4096), BF),
            pltpu.VMEM((224, 4096), BF),
            pltpu.VMEM((128, 4096), BF),
            pltpu.VMEM((8, 128, 128), BF),
            pltpu.VMEM((224, 512), BF),
            pltpu.VMEM((224, 256), BF),
            dma((4,)), dma((2,)), pltpu.SemaphoreType.REGULAR, pltpu.SemaphoreType.REGULAR,
            dma((3, 7)), dma((3, 7)), dma((3, 2, 4)), dma((3, 2, 4)),
            dma((3,)), dma((2,)), dma((8,)), dma((8,)),
            dma, dma,
            dma((2, 5, 3)), dma((2, 5, 3)), dma((4, 3)), dma((4, 3)),
        ],
        compiler_params=pltpu.CompilerParams(
            collective_id=0, has_side_effects=True, vmem_limit_bytes=60 * 1024 * 1024
        ),
        cost_estimate=pl.CostEstimate(flops=10**9, bytes_accessed=10**7, transcendentals=10**6),
    )(tokens.T, section_weights[0].T, up_weight.T, cotangent)
    return slot_t.T[None], up_t.T


def solution(mesh):
    placed = (P("dp", "tensor"), P("section", None, "tensor"), P(None, "tensor"), P("dp", None))
    return jax.shard_map(
        local,
        mesh=mesh,
        in_specs=placed,
        out_specs=(P("section", "dp", "tensor"), P(("section", "dp"), "tensor")),
        check_vma=False,
    )
```

```python
import jax
import jax.numpy as jnp
from jax import lax
from jax.experimental import pallas as pl
from jax.experimental.pallas import tpu as pltpu
from jax.sharding import PartitionSpec as P

MESH = pl.DeviceIdType.MESH
BF, F32, I32 = jnp.bfloat16, jnp.float32, jnp.int32
NT = (((1,), (1,)), ((), ()))


def mod8(v):
    return lax.rem(v + 16, 8)


def both(*conditions):
    out = conditions[0]
    for c in conditions[1:]:
        out = jnp.logical_and(out, c)
    return out


def kernel(
    tok, slot_w, up_w, cot,
    out_slot, out_up,
    x1, x2, x3, units, gh_v, wf, wd, cot_v, cot_t, res_slot, res_up,
    load_sem, local_sem, ready0, ready1,
    p1_send, p1_recv, ring_send, ring_recv,
    perm_send, perm_recv, scat_send, scat_recv,
    gh_send, gh_recv,
    z_send, z_recv, sib_send, sib_recv,
):
    s = lax.axis_index("section")
    t = lax.axis_index("tensor")
    dp = lax.axis_index("dp")
    y, x = t // 8, lax.rem(t, 8)
    zl, core = dp // 2, lax.rem(dp, 2)
    z = s * 4 + zl
    first, second = s == 0, s == 1
    sib = {"dp": zl * 2 + 1 - core}
    even = core == 0
    o_me = jnp.where(even, y, x)
    i_me = jnp.where(even, x, y)
    so = jnp.where(even, 8, 1)
    si = jnp.where(even, 1, 8)

    def when(*conditions):
        return pl.when(both(*conditions))

    def count(*conditions):
        return both(*conditions).astype(I32)

    def inner_dev(i):
        return {"tensor": o_me * so + i * si}

    def outer_dev(o):
        return {"tensor": o * so + i_me * si}

    def z_dev(zz, c=core):
        return {"section": zz // 4, "dp": lax.rem(zz, 4) * 2 + c}

    def remote(src, dst, ss, rs, dev):
        return pltpu.make_async_remote_copy(
            src_ref=src, dst_ref=dst, send_sem=ss, recv_sem=rs,
            device_id=dev, device_id_type=MESH,
        )

    def slot_at(d_core, yy, xx):
        return jnp.where(d_core == 0, yy, xx), jnp.where(d_core == 0, xx, yy)

    own1, own2, own3 = x1.at[o_me, i_me], x2.at[o_me, i_me], x3.at[o_me, i_me]
    ld_tok = pltpu.make_async_copy(tok, own1, load_sem.at[0])
    ld_tok.start()

    @when(first)
    def _():
        pltpu.make_async_copy(slot_w, wf, load_sem.at[1]).start()
        pltpu.make_async_copy(up_w, wd, load_sem.at[2]).start()

    @when(second)
    def _():
        pltpu.make_async_copy(cot, cot_v, load_sem.at[3]).start()
        pltpu.make_async_copy(slot_w, wd, load_sem.at[2]).start()

    perm_t, perm_d = dp * 8 + x, y
    perm_z = y // 2
    has_perm = both(first, y != dp)
    up_src_t = (s * 4 + dp // 2) * 8 + lax.rem(dp, 2) * 4 + x // 2
    up_src_z = y // 2
    up_recvs = jnp.logical_not(both(up_src_t == t, y == dp))
    up_dst_d = lax.rem(y, 4) * 2 + x // 4
    up_dst_z = up_dst_d // 2
    up_dst_x = [lax.rem(x, 4) * 2 + h for h in range(2)]
    up_dst_t = [dp * 8 + v for v in up_dst_x]
    up_from = y // 4 == s
    up_self = [both(up_from, v == t, up_dst_d == dp) for v in up_dst_t]
    up_sends = [both(up_from, jnp.logical_not(v)) for v in up_self]

    barrier = pltpu.get_barrier_semaphore()

    def tell(sem, dev):
        pl.semaphore_signal(sem, inc=1, device_id=dev, device_id_type=MESH)

    def wait_for(sem, number):
        @when(number > 0)
        def _():
            pl.semaphore_wait(sem, number)

    def answer(dev):
        @when(first)
        def _():
            tell(ready0, dev)

        @when(second)
        def _():
            tell(ready1, dev)

    for k in range(1, 8):
        tell(barrier, inner_dev(mod8(i_me + k)))
    for k in (1, -1, 2, -2):
        tell(barrier, outer_dev(mod8(o_me + k)))
    tell(barrier, sib)

    @when(first)
    def _():
        tell(barrier, {"section": 1})

    @when(first, jnp.logical_or(zl == 0, zl == 3))
    def _():
        tell(barrier, {"section": 1, "dp": (3 - zl) * 2 + core})

    @when(first, zl < 3)
    def _():
        tell(barrier, {"dp": dp + 2})

    for q in range(1, 4):
        @when(second, zl < q)
        def _():
            tell(barrier, {"dp": 2 * q})
            tell(barrier, {"dp": 2 * q + 1})

    @when(has_perm, perm_z >= zl)
    def _():
        tell(barrier, {"tensor": perm_t, "dp": perm_d})

    @when(up_recvs, up_src_z >= zl)
    def _():
        tell(barrier, {"tensor": up_src_t, "dp": y})

    for h in range(2):
        @when(up_sends[h], up_dst_z > zl)
        def _():
            tell(barrier, {"tensor": up_dst_t[h], "dp": up_dst_d})

    expected = 12 + count(first, zl > 0) + jnp.where(second, 1 + 2 * zl, 0)
    expected += count(second, jnp.logical_or(zl == 0, zl == 3))
    expected += count(has_perm, perm_z <= zl) + count(up_recvs, up_src_z < zl)
    for h in range(2):
        expected += count(up_sends[h], up_dst_z <= zl)

    half = pl.ds(pl.multiple_of(lax.rem(y, 2) * 64, 64), 64), pl.ds(pl.multiple_of(lax.rem(x, 2) * 64, 64), 64)

    @when(second)
    def _():
        pltpu.make_async_copy(cot, cot_v, load_sem.at[3]).wait()
        for g in range(8):
            pos = y if g % 2 == 0 else x
            lanes = pl.ds(pl.multiple_of(g * 512 + (pos // 2) * 128, 128), 128)
            cot_t[g] = cot_v[:, lanes].T
        pltpu.make_async_copy(slot_w, wd, load_sem.at[2]).wait()
        gh = lax.dot_general(wd[...], cot_v[...], NT, preferred_element_type=F32)
        gh_v[...] = gh.astype(BF)

    ld_tok.wait()
    pl.semaphore_wait(barrier, expected)

    @when(first, zl > 0)
    def _():
        tell(ready0, {"dp": dp - 2})

    for q in range(3):
        @when(second, zl > q)
        def _():
            tell(ready1, {"dp": 2 * q})
            tell(ready1, {"dp": 2 * q + 1})

    @when(second, jnp.logical_or(zl == 0, zl == 3))
    def _():
        tell(ready1, {"section": 0, "dp": (3 - zl) * 2 + core})

    @when(has_perm, perm_z < zl)
    def _():
        tell(ready0, {"tensor": perm_t, "dp": perm_d})

    @when(up_recvs, up_src_z < zl)
    def _():
        answer({"tensor": up_src_t, "dp": y})

    ups_above = count(up_sends[0], up_dst_z > zl) + count(up_sends[1], up_dst_z > zl)

    def p1_copy(buf, n, k):
        own = buf.at[o_me, i_me]
        return remote(own, own, p1_send.at[n, k - 1], p1_recv.at[n, k - 1],
                      inner_dev(mod8(i_me + k)))

    def ring_copy(buf, n, way, at):
        sign = 1 if way == 0 else -1
        part = buf.at[mod8(o_me - (0 if at < 2 else 2 * sign))]
        if at == 3:
            part = part.at[pl.ds(4 * way, 4)]
        return remote(part, part, ring_send.at[n, way, at], ring_recv.at[n, way, at],
                      outer_dev(mod8(o_me + sign * (1 + at % 2))))

    def p1_start(buf, n):
        for k in range(1, 8):
            p1_copy(buf, n, k).start()

    def p1_wait(buf, n):
        for k in range(1, 8):
            p1_copy(buf, n, k).wait_recv()

    def ring_first(buf, n):
        for at in (1, 0):
            for way in range(2):
                ring_copy(buf, n, way, at).start()

    def ring_second(buf, n):
        for way in range(2):
            ring_copy(buf, n, way, 1).wait_recv()
            ring_copy(buf, n, way, 3).start()
            ring_copy(buf, n, way, 2).start()

    def ring_rest(buf, n):
        for at in (0, 2, 3):
            for way in range(2):
                ring_copy(buf, n, way, at).wait_recv()

    def p1_sent(buf, n):
        for k in range(1, 8):
            p1_copy(buf, n, k).wait_send()

    def ring_sent(buf, n):
        for at in range(4):
            for way in range(2):
                ring_copy(buf, n, way, at).wait_send()

    def perm_copy():
        a, b = slot_at(lax.rem(y, 2), dp, x)
        return remote(own1, x2.at[a, b], perm_send.at[0], perm_recv.at[0],
                      {"tensor": perm_t, "dp": perm_d})

    def up_copy(h):
        a, b = slot_at(lax.rem(up_dst_d, 2), dp, up_dst_x[h])
        return remote(own1.at[pl.ds(32 * h, 32)], x3.at[a, b],
                      perm_send.at[1 + h], perm_recv.at[1],
                      {"tensor": up_dst_t[h], "dp": up_dst_d})

    def perm_local():
        return pltpu.make_async_copy(own1, own2, local_sem.at[0])

    def up_local(h):
        return pltpu.make_async_copy(own1.at[pl.ds(32 * h, 32)], own3, local_sem.at[1])

    def up_start():
        for h in range(2):
            @when(up_sends[h])
            def _():
                up_copy(h).start()

            @when(up_self[h])
            def _():
                up_local(h).start()

    def up_wait():
        @when(up_recvs)
        def _():
            up_copy(0).wait_recv()

        @when(jnp.logical_not(up_recvs))
        def _():
            up_local(0).wait()

    def scat_copy(g):
        place = x2.at[y if g % 2 == 0 else x, dp]
        return remote(cot_t.at[g, half[g % 2]], place, scat_send.at[g], scat_recv.at[dp], {"dp": g})

    def scat_local(g):
        place = x2.at[y if g % 2 == 0 else x, dp]
        return pltpu.make_async_copy(cot_t.at[g, half[g % 2]], place, local_sem.at[0])

    def scat_arrived(g):
        place = x2.at[o_me, g]
        return remote(place, place, scat_send.at[g], scat_recv.at[g], sib)

    def gh_copy():
        return remote(gh_v, gh_v, gh_send, gh_recv, {"section": 0})

    def z_rides(way, d, c, to):
        if way == 0:
            src = to - d
            ok = both(src >= 0, src < 4, jnp.logical_or(to < 4, src >= 2))
            on = src >= 2
        else:
            src = mod8(to + d)
            ok = both(src < 4, jnp.where(to < 4, src > to, src < 2))
            on = src < 2
        return both(ok, to < 4) if c == 0 else ok if c == 1 else both(ok, on)

    def z_copy(way, d, c):
        sign = 1 if way == 0 else -1
        src = mod8(z - sign * (d - 1))
        part = units.at[lax.rem(src, 4) * 2 + core, c]
        return remote(part, part, z_send.at[way, d - 1, c], z_recv.at[way, d - 1, c], z_dev(mod8(z + sign)))

    def z_sends(way, d, c):
        return z_rides(way, d, c, mod8(z + (1 if way == 0 else -1)))

    def z_sib(k, c):
        q = lax.rem(mod8(z + k), 4)
        unit = units.at[q * 2 + core, c]
        return remote(unit, unit, sib_send.at[q, c], sib_recv.at[q, c], sib)

    def z_wanted(c):
        return first if c == 0 else second if c == 2 else jnp.logical_or(first, second)

    def z_step(d):
        for c in (1, 0, 2):
            for way in range(2):
                if d > 1:
                    @when(z_rides(way, d - 1, c, z))
                    def _():
                        z_copy(way, d - 1, c).wait_recv()

                if d < 6:
                    @when(z_sends(way, d, c))
                    def _():
                        z_copy(way, d, c).start()

                if d > 1:
                    @when(z_rides(way, d - 1, c, z), z_wanted(c))
                    def _():
                        z_sib(1 - d if way == 0 else d - 1, c).start()

    @when(first)
    def _():
        p1_start(x1, 0)
        wait_for(ready0, count(zl < 3) + count(has_perm, perm_z > zl) + ups_above)

        @when(has_perm)
        def _():
            perm_copy().start()

        @when(y == dp)
        def _():
            perm_local().start()

        up_start()
        p1_wait(x1, 0)
        ring_first(x1, 0)
        ring_second(x1, 0)

        @when(has_perm)
        def _():
            perm_copy().wait_recv()

        @when(y == dp)
        def _():
            perm_local().wait()

        up_wait()
        p1_start(x2, 1)
        p1_start(x3, 2)
        p1_wait(x2, 1)
        ring_first(x2, 1)
        p1_wait(x3, 2)
        ring_first(x3, 2)
        ring_rest(x1, 0)
        pltpu.make_async_copy(slot_w, wf, load_sem.at[1]).wait()
        pltpu.make_async_copy(up_w, wd, load_sem.at[2]).wait()

        gate_pre = jnp.zeros((224, 128), F32)
        up_pre = jnp.zeros((224, 128), F32)
        for yy in range(8):
            places = [slot_at(core, yy, xx) for xx in range(8)]
            rows = jnp.concatenate([x1[a, b] for a, b in places], axis=0)
            gate_pre += jnp.dot(wf[:, yy * 512 : yy * 512 + 512], rows, preferred_element_type=F32)
            up_pre += jnp.dot(wd[:, yy * 512 : yy * 512 + 512], rows, preferred_element_type=F32)
        gh_copy().wait_recv()
        grad_hidden = gh_v[...].astype(F32)
        sg = jax.nn.sigmoid(gate_pre)
        act = gate_pre * sg
        units[dp, 1] = (grad_hidden * act).astype(BF)
        units[dp, 0] = (grad_hidden * up_pre * sg * (1.0 + gate_pre * (1.0 - sg))).astype(BF)
        units[dp, 2] = (act * up_pre).astype(BF)

        @when(jnp.logical_or(zl == 0, zl == 3))
        def _():
            pl.semaphore_wait(ready1, 1)

        z_step(1)
        z_sib(0, 1).start()
        z_sib(0, 0).start()
        z_step(2)
        ring_second(x2, 1)
        ring_second(x3, 2)
        z_step(3)
        z_step(4)

    @when(second)
    def _():
        gh_copy().start()
        wait_for(ready1, 2 * (3 - zl) + ups_above)
        up_start()
        for g in range(8):
            @when(dp != g)
            def _():
                scat_copy(g).start()

            @when(dp == g)
            def _():
                scat_local(g).start()
        up_wait()
        p1_start(x3, 2)
        for g in range(8):
            @when(dp != g)
            def _():
                scat_arrived(g).wait_recv()

            @when(dp == g)
            def _():
                scat_local(g).wait()
        ring_first(x2, 1)
        p1_wait(x3, 2)
        ring_first(x3, 2)
        ring_second(x2, 1)
        ring_second(x3, 2)
        for d in range(2, 7):
            z_step(d)

    ring_rest(x2, 1)
    ring_rest(x3, 2)
    side = jnp.where(first, 0, 2)
    for q in range(4):
        for c in (1, side):
            unit = units.at[q * 2 + 1 - core, c]
            remote(unit, unit, sib_send.at[q, c], sib_recv.at[q, c], sib).wait_recv()

    total_slot = jnp.zeros((224, 512), F32)
    total_up = jnp.zeros((224, 256), F32)
    by_group = both(first, even)
    for pair in range(4):
        lefts, ups, rows_slot, rows_up = [], [], [], []
        for g in (2 * pair, 2 * pair + 1):
            lefts.append(units[g, side])
            ups.append(units[g, 1])
            rows_slot.append(jnp.concatenate(
                [x2[jnp.where(by_group, g, j), jnp.where(by_group, j, g)] for j in range(8)], axis=0))
            places = [slot_at(core, g, xx) for xx in range(8)]
            rows_up.append(jnp.concatenate([x3[a, b] for a, b in places], axis=0))
        total_slot += lax.dot_general(
            jnp.concatenate(lefts, axis=1), jnp.concatenate(rows_slot, axis=1), NT,
            preferred_element_type=F32)
        total_up += lax.dot_general(
            jnp.concatenate(ups, axis=1), jnp.concatenate(rows_up, axis=1), NT,
            preferred_element_type=F32)
    res_slot[...] = total_slot.astype(BF)
    res_up[...] = total_up.astype(BF)
    st_slot = pltpu.make_async_copy(res_slot, out_slot, load_sem.at[0])
    st_up = pltpu.make_async_copy(res_up, out_up, load_sem.at[1])
    st_slot.start()
    st_up.start()

    @when(first)
    def _():
        p1_sent(x1, 0)
        ring_sent(x1, 0)
        p1_sent(x2, 1)

        @when(has_perm)
        def _():
            perm_copy().wait_send()

    @when(second)
    def _():
        for g in range(8):
            @when(dp != g)
            def _():
                scat_copy(g).wait_send()
        gh_copy().wait_send()

    ring_sent(x2, 1)
    p1_sent(x3, 2)
    ring_sent(x3, 2)
    for h in range(2):
        @when(up_sends[h])
        def _():
            up_copy(h).wait_send()
    for q in range(4):
        for c in (1, side):
            unit = units.at[q * 2 + core, c]
            remote(unit, unit, sib_send.at[q, c], sib_recv.at[q, c], sib).wait_send()
    for way in range(2):
        for d in range(1, 6):
            for c in range(3):
                @when(z_sends(way, d, c))
                def _():
                    z_copy(way, d, c).wait_send()
    st_slot.wait()
    st_up.wait()


def local(tokens, section_weights, up_weight, cotangent):
    dma = pltpu.SemaphoreType.DMA
    any_spec = pl.BlockSpec(memory_space=pl.ANY)
    slot_t, up_t = pl.pallas_call(
        kernel,
        out_shape=(jax.ShapeDtypeStruct((224, 512), BF), jax.ShapeDtypeStruct((224, 256), BF)),
        in_specs=[any_spec] * 4,
        out_specs=(any_spec, any_spec),
        scratch_shapes=[
            pltpu.VMEM((8, 8, 64, 128), BF),
            pltpu.VMEM((8, 8, 64, 128), BF),
            pltpu.VMEM((8, 8, 32, 128), BF),
            pltpu.VMEM((8, 3, 224, 128), BF),
            pltpu.VMEM((224, 128), BF),
            pltpu.VMEM((224, 4096), BF),
            pltpu.VMEM((224, 4096), BF),
            pltpu.VMEM((128, 4096), BF),
            pltpu.VMEM((8, 128, 128), BF),
            pltpu.VMEM((224, 512), BF),
            pltpu.VMEM((224, 256), BF),
            dma((4,)), dma((2,)), pltpu.SemaphoreType.REGULAR, pltpu.SemaphoreType.REGULAR,
            dma((3, 7)), dma((3, 7)), dma((3, 2, 4)), dma((3, 2, 4)),
            dma((3,)), dma((2,)), dma((8,)), dma((8,)),
            dma, dma,
            dma((2, 5, 3)), dma((2, 5, 3)), dma((4, 3)), dma((4, 3)),
        ],
        compiler_params=pltpu.CompilerParams(
            collective_id=0, has_side_effects=True, vmem_limit_bytes=60 * 1024 * 1024
        ),
        cost_estimate=pl.CostEstimate(flops=10**9, bytes_accessed=10**7, transcendentals=10**6),
    )(tokens.T, section_weights[0].T, up_weight.T, cotangent)
    return slot_t.T[None], up_t.T


def solution(mesh):
    placed = (P("dp", "tensor"), P("section", None, "tensor"), P(None, "tensor"), P("dp", None))
    return jax.shard_map(
        local,
        mesh=mesh,
        in_specs=placed,
        out_specs=(P("section", "dp", "tensor"), P(("section", "dp"), "tensor")),
        check_vma=False,
    )
```

```python
import jax
import jax.numpy as jnp
from jax import lax
from jax.experimental import pallas as pl
from jax.experimental.pallas import tpu as pltpu
from jax.sharding import PartitionSpec as P

MESH = pl.DeviceIdType.MESH
BF, F32, I32 = jnp.bfloat16, jnp.float32, jnp.int32
NT = (((1,), (1,)), ((), ()))


def mod8(v):
    return lax.rem(v + 16, 8)


def both(*conditions):
    out = conditions[0]
    for c in conditions[1:]:
        out = jnp.logical_and(out, c)
    return out


def kernel(
    tok, slot_w, up_w, cot,
    out_slot, out_up,
    x1, x2, x3, units, gh_v, wf, wd, cot_v, cot_t, res_slot, res_up,
    load_sem, local_sem, ready0, ready1,
    p1_send, p1_recv, ring_send, ring_recv,
    perm_send, perm_recv, scat_send, scat_recv,
    gh_send, gh_recv,
    z_send, z_recv, sib_send, sib_recv,
):
    s = lax.axis_index("section")
    t = lax.axis_index("tensor")
    dp = lax.axis_index("dp")
    y, x = t // 8, lax.rem(t, 8)
    zl, core = dp // 2, lax.rem(dp, 2)
    z = s * 4 + zl
    first, second = s == 0, s == 1
    sib = {"dp": zl * 2 + 1 - core}
    even = core == 0
    o_me = jnp.where(even, y, x)
    i_me = jnp.where(even, x, y)
    so = jnp.where(even, 8, 1)
    si = jnp.where(even, 1, 8)

    def when(*conditions):
        return pl.when(both(*conditions))

    def count(*conditions):
        return both(*conditions).astype(I32)

    def inner_dev(i):
        return {"tensor": o_me * so + i * si}

    def outer_dev(o):
        return {"tensor": o * so + i_me * si}

    def z_dev(zz, c=core):
        return {"section": zz // 4, "dp": lax.rem(zz, 4) * 2 + c}

    def remote(src, dst, ss, rs, dev):
        return pltpu.make_async_remote_copy(
            src_ref=src, dst_ref=dst, send_sem=ss, recv_sem=rs,
            device_id=dev, device_id_type=MESH,
        )

    def slot_at(d_core, yy, xx):
        return jnp.where(d_core == 0, yy, xx), jnp.where(d_core == 0, xx, yy)

    own1, own2, own3 = x1.at[o_me, i_me], x2.at[o_me, i_me], x3.at[o_me, i_me]
    ld_tok = pltpu.make_async_copy(tok, own1, load_sem.at[0])
    ld_tok.start()

    @when(first)
    def _():
        pltpu.make_async_copy(slot_w, wf, load_sem.at[1]).start()
        pltpu.make_async_copy(up_w, wd, load_sem.at[2]).start()

    @when(second)
    def _():
        pltpu.make_async_copy(cot, cot_v, load_sem.at[3]).start()
        pltpu.make_async_copy(slot_w, wd, load_sem.at[2]).start()

    perm_t, perm_d = dp * 8 + x, y
    perm_z = y // 2
    has_perm = both(first, y != dp)
    up_src_t = (s * 4 + dp // 2) * 8 + lax.rem(dp, 2) * 4 + x // 2
    up_src_z = y // 2
    up_recvs = jnp.logical_not(both(up_src_t == t, y == dp))
    up_dst_d = lax.rem(y, 4) * 2 + x // 4
    up_dst_z = up_dst_d // 2
    up_dst_x = [lax.rem(x, 4) * 2 + h for h in range(2)]
    up_dst_t = [dp * 8 + v for v in up_dst_x]
    up_from = y // 4 == s
    up_self = [both(up_from, v == t, up_dst_d == dp) for v in up_dst_t]
    up_sends = [both(up_from, jnp.logical_not(v)) for v in up_self]

    barrier = pltpu.get_barrier_semaphore()

    def tell(sem, dev):
        pl.semaphore_signal(sem, inc=1, device_id=dev, device_id_type=MESH)

    def wait_for(sem, number):
        @when(number > 0)
        def _():
            pl.semaphore_wait(sem, number)

    def answer(dev):
        @when(first)
        def _():
            tell(ready0, dev)

        @when(second)
        def _():
            tell(ready1, dev)

    for k in range(1, 8):
        tell(barrier, inner_dev(mod8(i_me + k)))
    for k in (1, -1, 2, -2):
        tell(barrier, outer_dev(mod8(o_me + k)))
    tell(barrier, sib)

    @when(first)
    def _():
        tell(barrier, {"section": 1})

    @when(first, jnp.logical_or(zl == 0, zl == 3))
    def _():
        tell(barrier, {"section": 1, "dp": (3 - zl) * 2 + core})

    @when(first, zl < 3)
    def _():
        tell(barrier, {"dp": dp + 2})

    for q in range(1, 4):
        @when(second, zl < q)
        def _():
            tell(barrier, {"dp": 2 * q})
            tell(barrier, {"dp": 2 * q + 1})

    @when(has_perm, perm_z >= zl)
    def _():
        tell(barrier, {"tensor": perm_t, "dp": perm_d})

    @when(up_recvs, up_src_z >= zl)
    def _():
        tell(barrier, {"tensor": up_src_t, "dp": y})

    for h in range(2):
        @when(up_sends[h], up_dst_z > zl)
        def _():
            tell(barrier, {"tensor": up_dst_t[h], "dp": up_dst_d})

    expected = 12 + count(first, zl > 0) + jnp.where(second, 1 + 2 * zl, 0)
    expected += count(second, jnp.logical_or(zl == 0, zl == 3))
    expected += count(has_perm, perm_z <= zl) + count(up_recvs, up_src_z < zl)
    for h in range(2):
        expected += count(up_sends[h], up_dst_z <= zl)

    half = pl.ds(pl.multiple_of(lax.rem(y, 2) * 64, 64), 64), pl.ds(pl.multiple_of(lax.rem(x, 2) * 64, 64), 64)

    @when(second)
    def _():
        pltpu.make_async_copy(cot, cot_v, load_sem.at[3]).wait()
        for g in range(8):
            pos = y if g % 2 == 0 else x
            lanes = pl.ds(pl.multiple_of(g * 512 + (pos // 2) * 128, 128), 128)
            cot_t[g] = cot_v[:, lanes].T
        pltpu.make_async_copy(slot_w, wd, load_sem.at[2]).wait()
        gh = lax.dot_general(wd[...], cot_v[...], NT, preferred_element_type=F32)
        gh_v[...] = gh.astype(BF)

    ld_tok.wait()
    pl.semaphore_wait(barrier, expected)

    @when(first, zl > 0)
    def _():
        tell(ready0, {"dp": dp - 2})

    for q in range(3):
        @when(second, zl > q)
        def _():
            tell(ready1, {"dp": 2 * q})
            tell(ready1, {"dp": 2 * q + 1})

    @when(second, jnp.logical_or(zl == 0, zl == 3))
    def _():
        tell(ready1, {"section": 0, "dp": (3 - zl) * 2 + core})

    @when(has_perm, perm_z < zl)
    def _():
        tell(ready0, {"tensor": perm_t, "dp": perm_d})

    @when(up_recvs, up_src_z < zl)
    def _():
        answer({"tensor": up_src_t, "dp": y})

    ups_above = count(up_sends[0], up_dst_z > zl) + count(up_sends[1], up_dst_z > zl)

    def p1_copy(buf, n, k):
        own = buf.at[o_me, i_me]
        return remote(own, own, p1_send.at[n, k - 1], p1_recv.at[n, k - 1],
                      inner_dev(mod8(i_me + k)))

    def ring_copy(buf, n, way, at):
        sign = 1 if way == 0 else -1
        part = buf.at[mod8(o_me - (0 if at < 2 else 2 * sign))]
        if at == 3:
            part = part.at[pl.ds(4 * way, 4)]
        return remote(part, part, ring_send.at[n, way, at], ring_recv.at[n, way, at],
                      outer_dev(mod8(o_me + sign * (1 + at % 2))))

    def p1_start(buf, n):
        for k in range(1, 8):
            p1_copy(buf, n, k).start()

    def p1_wait(buf, n):
        for k in range(1, 8):
            p1_copy(buf, n, k).wait_recv()

    def ring_first(buf, n):
        for at in (1, 0):
            for way in range(2):
                ring_copy(buf, n, way, at).start()

    def ring_second(buf, n):
        for way in range(2):
            ring_copy(buf, n, way, 1).wait_recv()
            ring_copy(buf, n, way, 3).start()
            ring_copy(buf, n, way, 2).start()

    def ring_rest(buf, n):
        for at in (0, 2, 3):
            for way in range(2):
                ring_copy(buf, n, way, at).wait_recv()

    def p1_sent(buf, n):
        for k in range(1, 8):
            p1_copy(buf, n, k).wait_send()

    def ring_sent(buf, n):
        for at in range(4):
            for way in range(2):
                ring_copy(buf, n, way, at).wait_send()

    def perm_copy():
        a, b = slot_at(lax.rem(y, 2), dp, x)
        return remote(own1, x2.at[a, b], perm_send.at[0], perm_recv.at[0],
                      {"tensor": perm_t, "dp": perm_d})

    def up_copy(h):
        a, b = slot_at(lax.rem(up_dst_d, 2), dp, up_dst_x[h])
        return remote(own1.at[pl.ds(32 * h, 32)], x3.at[a, b],
                      perm_send.at[1 + h], perm_recv.at[1],
                      {"tensor": up_dst_t[h], "dp": up_dst_d})

    def perm_local():
        return pltpu.make_async_copy(own1, own2, local_sem.at[0])

    def up_local(h):
        return pltpu.make_async_copy(own1.at[pl.ds(32 * h, 32)], own3, local_sem.at[1])

    def up_start():
        for h in range(2):
            @when(up_sends[h])
            def _():
                up_copy(h).start()

            @when(up_self[h])
            def _():
                up_local(h).start()

    def up_wait():
        @when(up_recvs)
        def _():
            up_copy(0).wait_recv()

        @when(jnp.logical_not(up_recvs))
        def _():
            up_local(0).wait()

    def scat_copy(g):
        place = x2.at[y if g % 2 == 0 else x, dp]
        return remote(cot_t.at[g, half[g % 2]], place, scat_send.at[g], scat_recv.at[dp], {"dp": g})

    def scat_local(g):
        place = x2.at[y if g % 2 == 0 else x, dp]
        return pltpu.make_async_copy(cot_t.at[g, half[g % 2]], place, local_sem.at[0])

    def scat_arrived(g):
        place = x2.at[o_me, g]
        return remote(place, place, scat_send.at[g], scat_recv.at[g], sib)

    def gh_copy():
        return remote(gh_v, gh_v, gh_send, gh_recv, {"section": 0})

    def z_rides(way, d, c, to):
        if way == 0:
            src = to - d
            ok = both(src >= 0, src < 4, jnp.logical_or(to < 4, src >= 2))
            on = src >= 2
        else:
            src = mod8(to + d)
            ok = both(src < 4, jnp.where(to < 4, src > to, src < 2))
            on = src < 2
        return both(ok, to < 4) if c == 0 else ok if c == 1 else both(ok, on)

    def z_copy(way, d, c):
        sign = 1 if way == 0 else -1
        src = mod8(z - sign * (d - 1))
        part = units.at[lax.rem(src, 4) * 2 + core, c]
        return remote(part, part, z_send.at[way, d - 1, c], z_recv.at[way, d - 1, c], z_dev(mod8(z + sign)))

    def z_sends(way, d, c):
        return z_rides(way, d, c, mod8(z + (1 if way == 0 else -1)))

    def z_sib(k, c):
        q = lax.rem(mod8(z + k), 4)
        unit = units.at[q * 2 + core, c]
        return remote(unit, unit, sib_send.at[q, c], sib_recv.at[q, c], sib)

    def z_wanted(c):
        return first if c == 0 else second if c == 2 else jnp.logical_or(first, second)

    def z_step(d):
        for c in (1, 0, 2):
            for way in range(2):
                if d > 1:
                    @when(z_rides(way, d - 1, c, z))
                    def _():
                        z_copy(way, d - 1, c).wait_recv()

                if d < 6:
                    @when(z_sends(way, d, c))
                    def _():
                        z_copy(way, d, c).start()

                if d > 1:
                    @when(z_rides(way, d - 1, c, z), z_wanted(c))
                    def _():
                        z_sib(1 - d if way == 0 else d - 1, c).start()

    @when(first)
    def _():
        p1_start(x1, 0)
        wait_for(ready0, count(zl < 3) + count(has_perm, perm_z > zl) + ups_above)

        @when(has_perm)
        def _():
            perm_copy().start()

        @when(y == dp)
        def _():
            perm_local().start()

        up_start()
        p1_wait(x1, 0)
        ring_first(x1, 0)
        ring_second(x1, 0)

        @when(has_perm)
        def _():
            perm_copy().wait_recv()

        @when(y == dp)
        def _():
            perm_local().wait()

        up_wait()
        p1_start(x2, 1)
        p1_start(x3, 2)
        p1_wait(x2, 1)
        ring_first(x2, 1)
        p1_wait(x3, 2)
        ring_first(x3, 2)
        ring_rest(x1, 0)
        pltpu.make_async_copy(slot_w, wf, load_sem.at[1]).wait()
        pltpu.make_async_copy(up_w, wd, load_sem.at[2]).wait()

        gate_pre = jnp.zeros((224, 128), F32)
        up_pre = jnp.zeros((224, 128), F32)
        for yy in range(8):
            places = [slot_at(core, yy, xx) for xx in range(8)]
            rows = jnp.concatenate([x1[a, b] for a, b in places], axis=0)
            gate_pre += jnp.dot(wf[:, yy * 512 : yy * 512 + 512], rows, preferred_element_type=F32)
            up_pre += jnp.dot(wd[:, yy * 512 : yy * 512 + 512], rows, preferred_element_type=F32)
        gh_copy().wait_recv()
        grad_hidden = gh_v[...].astype(F32)
        sg = jax.nn.sigmoid(gate_pre)
        act = gate_pre * sg
        units[dp, 1] = (grad_hidden * act).astype(BF)
        units[dp, 0] = (grad_hidden * up_pre * sg * (1.0 + gate_pre * (1.0 - sg))).astype(BF)
        units[dp, 2] = (act * up_pre).astype(BF)

        @when(jnp.logical_or(zl == 0, zl == 3))
        def _():
            pl.semaphore_wait(ready1, 1)

        z_step(1)
        z_sib(0, 1).start()
        z_sib(0, 0).start()
        z_step(2)
        ring_second(x2, 1)
        ring_second(x3, 2)
        z_step(3)
        z_step(4)

    @when(second)
    def _():
        gh_copy().start()
        wait_for(ready1, 2 * (3 - zl) + ups_above)
        up_start()
        for g in range(8):
            @when(dp != g)
            def _():
                scat_copy(g).start()

            @when(dp == g)
            def _():
                scat_local(g).start()
        up_wait()
        p1_start(x3, 2)
        for g in range(8):
            @when(dp != g)
            def _():
                scat_arrived(g).wait_recv()

            @when(dp == g)
            def _():
                scat_local(g).wait()
        ring_first(x2, 1)
        p1_wait(x3, 2)
        ring_first(x3, 2)
        ring_second(x2, 1)
        ring_second(x3, 2)
        for d in range(2, 7):
            z_step(d)

    ring_rest(x2, 1)
    side = jnp.where(first, 0, 2)
    for q in range(4):
        for c in (1, side):
            unit = units.at[q * 2 + 1 - core, c]
            remote(unit, unit, sib_send.at[q, c], sib_recv.at[q, c], sib).wait_recv()

    by_group = both(first, even)
    total_slot = jnp.zeros((224, 512), F32)
    for pair in range(4):
        groups = (2 * pair, 2 * pair + 1)
        rows = [
            jnp.concatenate(
                [x2[jnp.where(by_group, g, j), jnp.where(by_group, j, g)] for j in range(8)], axis=0)
            for g in groups
        ]
        total_slot += lax.dot_general(
            jnp.concatenate([units[g, side] for g in groups], axis=1),
            jnp.concatenate(rows, axis=1), NT, preferred_element_type=F32)
    res_slot[...] = total_slot.astype(BF)
    st_slot = pltpu.make_async_copy(res_slot, out_slot, load_sem.at[0])
    st_slot.start()

    ring_rest(x3, 2)
    total_up = jnp.zeros((224, 256), F32)
    for pair in range(4):
        groups = (2 * pair, 2 * pair + 1)
        rows = []
        for g in groups:
            places = [slot_at(core, g, xx) for xx in range(8)]
            rows.append(jnp.concatenate([x3[a, b] for a, b in places], axis=0))
        total_up += lax.dot_general(
            jnp.concatenate([units[g, 1] for g in groups], axis=1),
            jnp.concatenate(rows, axis=1), NT, preferred_element_type=F32)
    res_up[...] = total_up.astype(BF)
    st_up = pltpu.make_async_copy(res_up, out_up, load_sem.at[1])
    st_up.start()

    @when(first)
    def _():
        p1_sent(x1, 0)
        ring_sent(x1, 0)
        p1_sent(x2, 1)

        @when(has_perm)
        def _():
            perm_copy().wait_send()

    @when(second)
    def _():
        for g in range(8):
            @when(dp != g)
            def _():
                scat_copy(g).wait_send()
        gh_copy().wait_send()

    ring_sent(x2, 1)
    p1_sent(x3, 2)
    ring_sent(x3, 2)
    for h in range(2):
        @when(up_sends[h])
        def _():
            up_copy(h).wait_send()
    for q in range(4):
        for c in (1, side):
            unit = units.at[q * 2 + core, c]
            remote(unit, unit, sib_send.at[q, c], sib_recv.at[q, c], sib).wait_send()
    for way in range(2):
        for d in range(1, 6):
            for c in range(3):
                @when(z_sends(way, d, c))
                def _():
                    z_copy(way, d, c).wait_send()
    st_slot.wait()
    st_up.wait()


def local(tokens, section_weights, up_weight, cotangent):
    dma = pltpu.SemaphoreType.DMA
    any_spec = pl.BlockSpec(memory_space=pl.ANY)
    slot_t, up_t = pl.pallas_call(
        kernel,
        out_shape=(jax.ShapeDtypeStruct((224, 512), BF), jax.ShapeDtypeStruct((224, 256), BF)),
        in_specs=[any_spec] * 4,
        out_specs=(any_spec, any_spec),
        scratch_shapes=[
            pltpu.VMEM((8, 8, 64, 128), BF),
            pltpu.VMEM((8, 8, 64, 128), BF),
            pltpu.VMEM((8, 8, 32, 128), BF),
            pltpu.VMEM((8, 3, 224, 128), BF),
            pltpu.VMEM((224, 128), BF),
            pltpu.VMEM((224, 4096), BF),
            pltpu.VMEM((224, 4096), BF),
            pltpu.VMEM((128, 4096), BF),
            pltpu.VMEM((8, 128, 128), BF),
            pltpu.VMEM((224, 512), BF),
            pltpu.VMEM((224, 256), BF),
            dma((4,)), dma((2,)), pltpu.SemaphoreType.REGULAR, pltpu.SemaphoreType.REGULAR,
            dma((3, 7)), dma((3, 7)), dma((3, 2, 4)), dma((3, 2, 4)),
            dma((3,)), dma((2,)), dma((8,)), dma((8,)),
            dma, dma,
            dma((2, 5, 3)), dma((2, 5, 3)), dma((4, 3)), dma((4, 3)),
        ],
        compiler_params=pltpu.CompilerParams(
            collective_id=0, has_side_effects=True, vmem_limit_bytes=60 * 1024 * 1024
        ),
        cost_estimate=pl.CostEstimate(flops=10**9, bytes_accessed=10**7, transcendentals=10**6),
    )(tokens.T, section_weights[0].T, up_weight.T, cotangent)
    return slot_t.T[None], up_t.T


def solution(mesh):
    placed = (P("dp", "tensor"), P("section", None, "tensor"), P(None, "tensor"), P("dp", None))
    return jax.shard_map(
        local,
        mesh=mesh,
        in_specs=placed,
        out_specs=(P("section", "dp", "tensor"), P(("section", "dp"), "tensor")),
        check_vma=False,
    )
```
